512 devices in a mesh: prow: 16 (over x, y_lo, core), pcol: 32 (over y_hi, z).
Axes of the slice: x: 4, y: 4 (y_hi: 2, y_lo: 2; y = y_hi * 2 + y_lo), z: 16, core: 2. Of those that a mesh axis runs over, the one named last changes fastest.
Arguments:
- mantissa: bfloat16 [20480, 1024], P(('pcol', 'prow')), may hold values from -0.5 to 0.5
- exponent: int32 [20480, 8], P(('pcol', 'prow')), may hold values from -2 to 2
- occ_level: int32 [1024], replicated, may hold values from -300 to -21
- virt_level: int32 [1024], replicated, may hold values from 50 to 399
Outputs:
- response: float32 [20480, 20480], P('prow', 'pcol')
The draws below stay inside these ranges and needn't reach their ends.
All inputs are finite; a program needn't handle non-finite values.
Results may differ from the reference program's by a relative error of at most 0.00064.
Values may be sent and summed in bfloat16 or wider, within the bound.
No kernel may reach another device: no remote copies, remote signals or barrier semaphores. Data moves between devices by JAX's collectives and lax.ppermute only.
A program may use at most 64 MiB of HBM per device.

```python
import jax
import jax.numpy as jnp
from jax import lax

K = 1024
NAUX = 20480
KBLK = 8


def set_ends(entries, key, low, largest):
    dims = entries.shape
    spot = [jax.random.randint(jax.random.fold_in(key, axis), (), 0, dims[axis]) for axis in range(len(dims))]
    entries = entries.at[tuple(spot)].set(low)
    longest = dims.index(max(dims))
    spot[longest] = (spot[longest] + 1) % dims[longest]
    return entries.at[tuple(spot)].set(largest)


def levels(key, extent, shards, low, largest):
    loudness, own = 1.0, jax.random.fold_in(key, 6)
    for position, parts in shards:
        draws = jnp.exp(jax.random.uniform(jax.random.fold_in(own, position), (parts,), jnp.float32, low / len(shards), largest / len(shards)))
        loudness = loudness * jnp.repeat(draws, extent[position] // parts).reshape([-1 if axis == position else 1 for axis in range(len(extent))])
    return loudness


def centred(own_key, extent, scale, limit, split=(), dtype=jnp.bfloat16):
    array = scale * jax.random.normal(own_key, extent, jnp.float32)
    if split:
        array = array * levels(own_key, extent, split, -0.22, 0.18)
    return jnp.clip(array, -limit, limit).astype(dtype)


def setup_inputs(seed: int = 0) -> dict:
    key_of = jax.random.split(jax.random.key(seed), 5)
    mantissa = centred(key_of[0], (NAUX, K), (K ** -0.5), 0.5, ((0, 512),))
    exponent = set_ends(jax.random.randint(key_of[1], (NAUX, KBLK), -2, 3), jax.random.fold_in(key_of[1], 1), -2, 2).astype(jnp.int32)
    occ_level = set_ends(jax.random.randint(key_of[2], (K,), -300, -20), jax.random.fold_in(key_of[2], 1), -300, (-20) - 1).astype(jnp.int32)
    virt_level = set_ends(jax.random.randint(key_of[3], (K,), 50, 400), jax.random.fold_in(key_of[3], 1), 50, 399).astype(jnp.int32)
    return {"mantissa": mantissa, "exponent": exponent, "occ_level": occ_level, "virt_level": virt_level}


def dequantize(mantissa, exponent):
    block_scale = jnp.exp2(exponent.astype(jnp.float32))
    full_scale = jnp.repeat(block_scale, 128, axis=1)
    return (mantissa.astype(jnp.float32) * full_scale).astype(jnp.bfloat16)


def pair_weights(occ_level, virt_level):
    energy_gap = 0.01 * (virt_level - occ_level).astype(jnp.float32)
    return -4.0 * energy_gap / (energy_gap * energy_gap + 1.0)


def reference(mantissa, exponent, occ_level, virt_level):
    factor = dequantize(mantissa, exponent)
    weights = pair_weights(occ_level, virt_level)
    scaled = (factor.astype(jnp.float32) * weights[None, :]).astype(jnp.bfloat16)
    return lax.dot_general(factor, scaled, (((1,), (1,)), ((), ())), preferred_element_type=jnp.float32)
```

```python
import jax
import jax.numpy as jnp
from jax import lax
from jax.experimental import pallas as pl
from jax.experimental.pallas import tpu as pltpu
from jax.sharding import PartitionSpec as P

NX, NY, NZ = 4, 4, 16
ROWS = 160
CHUNKS = 8
DEPTH = 1024
COLS = 640
JOINT = ("prow", "pcol")
LIMIT = 32 * 1024 * 1024


def split(index):
    row, col = divmod(index, 2 * NZ)
    return row >> 2, (col // NZ) * 2 + ((row >> 1) & 1), col % NZ, row & 1


def join(x, y, z, core):
    x, y, z = x % NX, y % NY, z % NZ
    return (x * 4 + (y & 1) * 2 + core) * 2 * NZ + (y >> 1) * NZ + z


def shift(dx=0, dy=0, dz=0):
    pairs = []
    for source in range(2 * NX * NY * NZ):
        x, y, z, core = split(source)
        pairs.append((source, join(x + dx, y + dy, z + dz, core)))
    return pairs


def spread():
    pairs = []
    for source in range(2 * NX * NY * NZ):
        x, y, z, core = split(source)
        col = (y >> 1) * NZ + z
        row, half = col // 2, col % 2
        chunk = 4 * half + x
        y_hi = (y & 1) ^ ((row >> 1) & 1)
        z_to = (chunk - 4 * y_hi + 2 * row) % 8 + 8 * core
        pairs.append((source, row * 2 * NZ + y_hi * NZ + z_to))
    return pairs


def send(block, pairs):
    return lax.ppermute(block, JOINT, pairs)


def dequantize_body(mantissa, exponent, out):
    scale = jnp.exp2(exponent[...].astype(jnp.float32))
    for k in range(DEPTH // 128):
        span = slice(128 * k, 128 * (k + 1))
        out[:, span] = (mantissa[:, span].astype(jnp.float32) * scale[:, k : k + 1]).astype(jnp.bfloat16)


def dequantize(mantissa, exponent):
    return pl.pallas_call(
        dequantize_body,
        out_shape=jax.ShapeDtypeStruct(mantissa.shape, jnp.bfloat16),
        compiler_params=pltpu.CompilerParams(vmem_limit_bytes=LIMIT),
    )(mantissa, exponent)


def scale_body(place, weights, own, before, after, across, out):
    for step, block in ((0, own), (3, before), (1, after), (2, across)):
        start = pl.multiple_of(lax.rem(place[0] + step, 4) * ROWS, ROWS)
        out[pl.ds(start, ROWS), :] = (block[...].astype(jnp.float32) * weights[...]).astype(jnp.bfloat16)


def scale(place, weights, own, before, after, across):
    whole = pl.BlockSpec(memory_space=pltpu.VMEM)
    return pl.pallas_call(
        scale_body,
        out_shape=jax.ShapeDtypeStruct((COLS, DEPTH), jnp.bfloat16),
        in_specs=[pl.BlockSpec(memory_space=pltpu.SMEM)] + [whole] * 5,
        out_specs=whole,
        compiler_params=pltpu.CompilerParams(vmem_limit_bytes=LIMIT),
        cost_estimate=pl.CostEstimate(flops=COLS * DEPTH, bytes_accessed=4 * COLS * DEPTH, transcendentals=0),
    )(place, weights, own, before, after, across)


def multiply_body(colors, rows, columns, *rest):
    out = rest[-1]
    out[0] = lax.dot_general(
        rows[...], columns[...], (((1,), (1,)), ((), ())), preferred_element_type=jnp.float32
    )


def multiply(colors, rows, columns, response):
    count = rows.shape[0] // ROWS
    in_specs = [
        pl.BlockSpec((ROWS, DEPTH), lambda i, colors: (i, 0)),
        pl.BlockSpec((COLS, DEPTH), lambda i, colors: (0, 0)),
    ]
    args = [colors, rows, columns]
    aliases = {}
    if response is not None:
        in_specs.append(pl.BlockSpec(memory_space=pl.ANY))
        args.append(response)
        aliases = {3: 0}
    return pl.pallas_call(
        multiply_body,
        out_shape=jax.ShapeDtypeStruct((CHUNKS, ROWS, COLS), jnp.float32),
        grid_spec=pltpu.PrefetchScalarGridSpec(
            num_scalar_prefetch=1,
            grid=(count,),
            in_specs=in_specs,
            out_specs=pl.BlockSpec((1, ROWS, COLS), lambda i, colors: (colors[i], 0, 0)),
        ),
        input_output_aliases=aliases,
        compiler_params=pltpu.CompilerParams(vmem_limit_bytes=LIMIT),
        cost_estimate=pl.CostEstimate(
            flops=2 * count * ROWS * COLS * DEPTH,
            bytes_accessed=count * ROWS * (2 * DEPTH + 4 * COLS) + 2 * COLS * DEPTH,
            transcendentals=0,
        ),
    )(*args)


def pair_weights(occ_level, virt_level):
    energy_gap = 0.01 * (virt_level - occ_level).astype(jnp.float32)
    return -4.0 * energy_gap / (energy_gap * energy_gap + 1.0)


def per_device(mantissa, exponent, occ_level, virt_level):
    row, col = lax.axis_index("prow"), lax.axis_index("pcol")
    color = (col % NZ + 4 * (col // NZ) - 2 * row) % CHUNKS

    own = dequantize(mantissa, exponent)
    same_x = [[4 * x + i for i in range(4)] for x in range(NX)]
    group = lax.all_gather(own, "prow", axis=0, tiled=True, axis_index_groups=same_x)

    placed = send(group, spread())
    before = send(group, shift(dx=1))
    after = send(group, shift(dx=-1))
    across = send(group, shift(dx=2))

    down = send(placed, shift(dz=1))
    up = send(placed, shift(dz=-1))
    near = jnp.concatenate([placed, down, up], axis=0)
    far = send(near, shift(dy=2))
    down_two = send(down, shift(dz=1))
    up_two = send(up, shift(dz=-1))

    weights = pair_weights(occ_level, virt_level)[None, :]
    columns = scale((row // 4)[None], weights, group, before, after, across)

    def colors(*steps):
        return (color + jnp.array(steps, jnp.int32)) % CHUNKS

    response = multiply(colors(0, 7, 1), near, columns, None)
    response = multiply(colors(6), down_two, columns, response)
    response = multiply(colors(2), up_two, columns, response)
    response = multiply(colors(4, 3, 5), far, columns, response)
    return response.reshape(CHUNKS * ROWS, COLS)


def solution(mesh):
    return jax.shard_map(
        per_device,
        mesh=mesh,
        in_specs=(P(("pcol", "prow"), None), P(("pcol", "prow"), None), P(), P()),
        out_specs=P("prow", "pcol"),
        check_vma=False,
    )
```

```python
import jax
import jax.numpy as jnp
import numpy as np
from jax import lax
from jax.experimental import pallas as pl
from jax.experimental.pallas import tpu as pltpu
from jax.sharding import PartitionSpec as P

NX, NY, NZ = 4, 4, 16
ROWS = 160
CHUNKS = 8
DEPTH = 1024
COLS = 640
JOINT = ("prow", "pcol")
LIMIT = 32 * 1024 * 1024

PLACES = (
    (9, 1, 21, 29, 2, 10, 22, 30, 14, 6, 26, 18, 5, 13, 25, 17, 12, 4, 24, 16, 0, 8, 20, 28, 7, 15, 19, 27, 3, 11, 31, 23),
    (8, 0, 28, 20, 4, 12, 24, 16, 11, 3, 31, 23, 7, 15, 27, 19, 6, 14, 26, 18, 1, 9, 21, 29, 13, 5, 17, 25, 10, 2, 22, 30),
    (18, 26, 14, 6, 30, 22, 10, 2, 17, 25, 5, 13, 29, 21, 1, 9, 23, 31, 11, 3, 19, 27, 15, 7, 28, 20, 0, 8, 24, 16, 12, 4),
    (19, 27, 7, 15, 23, 31, 3, 11, 16, 24, 12, 4, 28, 20, 8, 0, 18, 26, 6, 14, 21, 29, 9, 1, 30, 22, 2, 10, 25, 17, 5, 13),
    (13, 5, 17, 25, 9, 1, 29, 21, 2, 10, 22, 30, 14, 6, 18, 26, 12, 4, 16, 24, 8, 0, 28, 20, 11, 3, 23, 31, 15, 7, 27, 19),
    (15, 7, 19, 27, 3, 11, 31, 23, 0, 8, 28, 20, 12, 4, 24, 16, 13, 5, 25, 17, 6, 14, 18, 26, 1, 9, 21, 29, 2, 10, 30, 22),
    (18, 26, 14, 6, 17, 25, 5, 13, 29, 21, 1, 9, 22, 30, 10, 2, 16, 24, 4, 12, 20, 28, 8, 0, 31, 23, 3, 11, 19, 27, 15, 7),
    (19, 27, 15, 7, 31, 23, 3, 11, 28, 20, 8, 0, 16, 24, 12, 4, 22, 30, 10, 2, 21, 29, 9, 1, 26, 18, 14, 6, 25, 17, 13, 5),
    (22, 30, 2, 10, 21, 29, 9, 1, 26, 18, 14, 6, 17, 25, 5, 13, 27, 19, 7, 15, 31, 23, 11, 3, 24, 16, 12, 4, 28, 20, 0, 8),
    (28, 20, 8, 0, 27, 19, 15, 7, 31, 23, 11, 3, 16, 24, 4, 12, 18, 26, 14, 6, 17, 25, 5, 13, 30, 22, 2, 10, 29, 21, 9, 1),
    (1, 9, 29, 21, 6, 14, 26, 18, 13, 5, 17, 25, 2, 10, 30, 22, 8, 0, 20, 28, 4, 12, 24, 16, 11, 3, 31, 23, 15, 7, 27, 19),
    (15, 7, 19, 27, 8, 0, 20, 28, 4, 12, 24, 16, 11, 3, 31, 23, 10, 2, 30, 22, 5, 13, 25, 17, 14, 6, 26, 18, 9, 1, 21, 29),
    (21, 29, 9, 1, 18, 26, 6, 14, 25, 17, 13, 5, 22, 30, 2, 10, 24, 16, 12, 4, 23, 31, 11, 3, 27, 19, 7, 15, 20, 28, 8, 0),
    (27, 19, 7, 15, 20, 28, 0, 8, 16, 24, 12, 4, 23, 31, 3, 11, 30, 22, 10, 2, 17, 25, 5, 13, 18, 26, 14, 6, 21, 29, 1, 9),
    (9, 1, 29, 21, 6, 14, 26, 18, 5, 13, 17, 25, 2, 10, 22, 30, 7, 15, 27, 19, 11, 3, 23, 31, 4, 12, 24, 16, 0, 8, 20, 28),
    (12, 4, 16, 24, 8, 0, 28, 20, 7, 15, 27, 19, 11, 3, 31, 23, 13, 5, 17, 25, 10, 2, 30, 22, 1, 9, 21, 29, 14, 6, 26, 18),
)


def color_of(row, col):
    return (col % NZ + 4 * (col // NZ) - 2 * row) % CHUNKS


def chunk_table():
    table = np.zeros((16, CHUNKS), np.int32)
    for row, places in enumerate(PLACES):
        for slot, col in enumerate(places):
            table[row, color_of(row, col)] = slot // 4
    return table


def split(index):
    row, col = divmod(index, 2 * NZ)
    return row >> 2, (col // NZ) * 2 + ((row >> 1) & 1), col % NZ, row & 1


def join(x, y, z, core):
    x, y, z = x % NX, y % NY, z % NZ
    return (x * 4 + (y & 1) * 2 + core) * 2 * NZ + (y >> 1) * NZ + z


def shift(dx=0, dy=0, dz=0):
    pairs = []
    for source in range(2 * NX * NY * NZ):
        x, y, z, core = split(source)
        pairs.append((source, join(x + dx, y + dy, z + dz, core)))
    return pairs


def spread():
    pairs = []
    for source in range(2 * NX * NY * NZ):
        x, y, z, core = split(source)
        col = (y >> 1) * NZ + z
        row, half = col // 2, col % 2
        place = PLACES[row][4 * (4 * half + x) + 2 * (y & 1) + core]
        pairs.append((source, row * 2 * NZ + place))
    return pairs


def flip_core():
    return [(source, source ^ (2 * NZ)) for source in range(2 * NX * NY * NZ)]


def send(block, pairs):
    return lax.ppermute(block, JOINT, pairs)


def hold_body(block, out):
    pass


def hold(block):
    anywhere = pl.BlockSpec(memory_space=pl.ANY)
    return pl.pallas_call(
        hold_body,
        out_shape=jax.ShapeDtypeStruct(block.shape, block.dtype),
        in_specs=[anywhere],
        out_specs=anywhere,
        input_output_aliases={0: 0},
        cost_estimate=pl.CostEstimate(flops=10**10, bytes_accessed=10**7, transcendentals=0),
    )(block)


def dequantize_body(mantissa_ref, exponent_ref, out, mantissa, exponent, sems):
    first = pltpu.make_async_copy(mantissa_ref, mantissa, sems.at[0])
    second = pltpu.make_async_copy(exponent_ref, exponent, sems.at[1])
    first.start()
    second.start()
    second.wait()
    scale = jnp.exp2(exponent[...].astype(jnp.float32))
    first.wait()
    for k in range(DEPTH // 128):
        span = slice(128 * k, 128 * (k + 1))
        out[:, span] = (mantissa[:, span].astype(jnp.float32) * scale[:, k : k + 1]).astype(jnp.bfloat16)


def dequantize(mantissa, exponent):
    anywhere = pl.BlockSpec(memory_space=pltpu.HBM)
    return pl.pallas_call(
        dequantize_body,
        out_shape=jax.ShapeDtypeStruct(mantissa.shape, jnp.bfloat16),
        in_specs=[anywhere, anywhere],
        out_specs=pl.BlockSpec(memory_space=pltpu.VMEM),
        scratch_shapes=[
            pltpu.VMEM(mantissa.shape, mantissa.dtype),
            pltpu.VMEM(exponent.shape, exponent.dtype),
            pltpu.SemaphoreType.DMA((2,)),
        ],
        compiler_params=pltpu.CompilerParams(vmem_limit_bytes=LIMIT),
    )(mantissa, exponent)


def multiply_body(first, order, columns, *rest):
    *blocks, response, held, sems = rest
    copies = []
    for block in blocks:
        for k in range(block.shape[0] // ROWS):
            slot = len(copies)
            held[slot] = lax.dot_general(
                block[ROWS * k : ROWS * (k + 1), :],
                columns[...],
                (((1,), (1,)), ((), ())),
                preferred_element_type=jnp.float32,
            )
            copies.append(pltpu.make_async_copy(held.at[slot], response.at[order[first + slot]], sems.at[slot]))
            copies[-1].start()
    for copy in copies:
        copy.wait()


def multiply(first, order, columns, blocks, response):
    count = sum(block.shape[0] for block in blocks) // ROWS
    whole = pl.BlockSpec(memory_space=pltpu.VMEM)
    anywhere = pl.BlockSpec(memory_space=pl.ANY)
    in_specs = [pl.BlockSpec(memory_space=pltpu.SMEM)] + [whole] * (1 + len(blocks))
    args = [order, columns, *blocks]
    aliases = {}

    def body(*refs):
        if response is not None:
            refs = refs[: len(args) - 1] + refs[len(args) :]
        multiply_body(first, *refs)

    if response is not None:
        in_specs.append(anywhere)
        args.append(response)
        aliases = {len(args) - 1: 0}
    return pl.pallas_call(
        body,
        out_shape=jax.ShapeDtypeStruct((CHUNKS, ROWS, COLS), jnp.float32),
        in_specs=in_specs,
        out_specs=anywhere,
        scratch_shapes=[pltpu.VMEM((count, ROWS, COLS), jnp.float32), pltpu.SemaphoreType.DMA((count,))],
        input_output_aliases=aliases,
        compiler_params=pltpu.CompilerParams(vmem_limit_bytes=LIMIT),
        cost_estimate=pl.CostEstimate(flops=count * ROWS, bytes_accessed=count * ROWS, transcendentals=0),
    )(*args)


def pair_weights(occ_level, virt_level):
    energy_gap = 0.01 * (virt_level - occ_level).astype(jnp.float32)
    return -4.0 * energy_gap / (energy_gap * energy_gap + 1.0)


def per_device(mantissa, exponent, occ_level, virt_level):
    row, col = lax.axis_index("prow"), lax.axis_index("pcol")

    own = dequantize(mantissa, exponent)
    same_x = [[4 * x + i for i in range(4)] for x in range(NX)]
    group = lax.all_gather(own, "prow", axis=0, tiled=True, axis_index_groups=same_x)

    placed = hold(send(group, spread()))
    same_core = [[2 * i + core for i in range(8)] for core in range(2)]
    eight = lax.all_to_all(
        jnp.broadcast_to(own, (8, *own.shape)), "prow", 0, 0, axis_index_groups=same_core
    )

    other = send(eight, flip_core())
    down = send(placed, shift(dz=1))
    up = send(placed, shift(dz=-1))
    over = send(placed, shift(dy=2))
    weights = pair_weights(occ_level, virt_level)
    first = jnp.where(row % 2 == 0, eight, other)
    second = jnp.where(row % 2 == 0, other, eight)
    columns = jnp.stack([first, second], axis=1).reshape(COLS, DEPTH)
    columns = (columns.astype(jnp.float32) * weights[None, :]).astype(jnp.bfloat16)
    steps = jnp.array([0, 7, 1, 4, 6, 2, 3, 5], jnp.int32)
    order = jnp.take(jnp.asarray(chunk_table()), row * CHUNKS + (color_of(row, col) + steps) % CHUNKS)
    down, up, over, columns, order = lax.optimization_barrier((down, up, over, columns, order))
    sides = jnp.concatenate([down, up], axis=0)
    over_sides = send(sides, shift(dy=2))
    down_two = send(down, shift(dz=1))
    up_two = send(up, shift(dz=-1))

    response = multiply(0, order, columns, [placed, down, up], None)
    response = multiply(3, order, columns, [over, down_two, up_two], response)
    response = multiply(6, order, columns, [over_sides], response)
    return response.reshape(CHUNKS * ROWS, COLS)


def solution(mesh):
    return jax.shard_map(
        per_device,
        mesh=mesh,
        in_specs=(P(("pcol", "prow"), None), P(("pcol", "prow"), None), P(), P()),
        out_specs=P("prow", "pcol"),
        check_vma=False,
    )
```

```python
import jax
import jax.numpy as jnp
import numpy as np
from jax import lax
from jax.experimental import pallas as pl
from jax.experimental.pallas import tpu as pltpu
from jax.sharding import PartitionSpec as P

NX, NY, NZ = 4, 4, 16
ROWS = 160
CHUNKS = 8
DEPTH = 1024
COLS = 640
JOINT = ("prow", "pcol")
LIMIT = 32 * 1024 * 1024

PLACES = (
    (9, 1, 21, 29, 2, 10, 22, 30, 14, 6, 26, 18, 5, 13, 25, 17, 12, 4, 24, 16, 0, 8, 20, 28, 7, 15, 19, 27, 3, 11, 31, 23),
    (8, 0, 28, 20, 4, 12, 24, 16, 11, 3, 31, 23, 7, 15, 27, 19, 6, 14, 26, 18, 1, 9, 21, 29, 13, 5, 17, 25, 10, 2, 22, 30),
    (18, 26, 14, 6, 30, 22, 10, 2, 17, 25, 5, 13, 29, 21, 1, 9, 23, 31, 11, 3, 19, 27, 15, 7, 28, 20, 0, 8, 24, 16, 12, 4),
    (19, 27, 7, 15, 23, 31, 3, 11, 16, 24, 12, 4, 28, 20, 8, 0, 18, 26, 6, 14, 21, 29, 9, 1, 30, 22, 2, 10, 25, 17, 5, 13),
    (13, 5, 17, 25, 9, 1, 29, 21, 2, 10, 22, 30, 14, 6, 18, 26, 12, 4, 16, 24, 8, 0, 28, 20, 11, 3, 23, 31, 15, 7, 27, 19),
    (15, 7, 19, 27, 3, 11, 31, 23, 0, 8, 28, 20, 12, 4, 24, 16, 13, 5, 25, 17, 6, 14, 18, 26, 1, 9, 21, 29, 2, 10, 30, 22),
    (18, 26, 14, 6, 17, 25, 5, 13, 29, 21, 1, 9, 22, 30, 10, 2, 16, 24, 4, 12, 20, 28, 8, 0, 31, 23, 3, 11, 19, 27, 15, 7),
    (19, 27, 15, 7, 31, 23, 3, 11, 28, 20, 8, 0, 16, 24, 12, 4, 22, 30, 10, 2, 21, 29, 9, 1, 26, 18, 14, 6, 25, 17, 13, 5),
    (22, 30, 2, 10, 21, 29, 9, 1, 26, 18, 14, 6, 17, 25, 5, 13, 27, 19, 7, 15, 31, 23, 11, 3, 24, 16, 12, 4, 28, 20, 0, 8),
    (28, 20, 8, 0, 27, 19, 15, 7, 31, 23, 11, 3, 16, 24, 4, 12, 18, 26, 14, 6, 17, 25, 5, 13, 30, 22, 2, 10, 29, 21, 9, 1),
    (1, 9, 29, 21, 6, 14, 26, 18, 13, 5, 17, 25, 2, 10, 30, 22, 8, 0, 20, 28, 4, 12, 24, 16, 11, 3, 31, 23, 15, 7, 27, 19),
    (15, 7, 19, 27, 8, 0, 20, 28, 4, 12, 24, 16, 11, 3, 31, 23, 10, 2, 30, 22, 5, 13, 25, 17, 14, 6, 26, 18, 9, 1, 21, 29),
    (21, 29, 9, 1, 18, 26, 6, 14, 25, 17, 13, 5, 22, 30, 2, 10, 24, 16, 12, 4, 23, 31, 11, 3, 27, 19, 7, 15, 20, 28, 8, 0),
    (27, 19, 7, 15, 20, 28, 0, 8, 16, 24, 12, 4, 23, 31, 3, 11, 30, 22, 10, 2, 17, 25, 5, 13, 18, 26, 14, 6, 21, 29, 1, 9),
    (9, 1, 29, 21, 6, 14, 26, 18, 5, 13, 17, 25, 2, 10, 22, 30, 7, 15, 27, 19, 11, 3, 23, 31, 4, 12, 24, 16, 0, 8, 20, 28),
    (12, 4, 16, 24, 8, 0, 28, 20, 7, 15, 27, 19, 11, 3, 31, 23, 13, 5, 17, 25, 10, 2, 30, 22, 1, 9, 21, 29, 14, 6, 26, 18),
)


def color_of(row, col):
    return (col % NZ + 4 * (col // NZ) - 2 * row) % CHUNKS


def chunk_table():
    table = np.zeros((16, CHUNKS), np.int32)
    for row, places in enumerate(PLACES):
        for slot, col in enumerate(places):
            table[row, color_of(row, col)] = slot // 4
    return table


def split(index):
    row, col = divmod(index, 2 * NZ)
    return row >> 2, (col // NZ) * 2 + ((row >> 1) & 1), col % NZ, row & 1


def join(x, y, z, core):
    x, y, z = x % NX, y % NY, z % NZ
    return (x * 4 + (y & 1) * 2 + core) * 2 * NZ + (y >> 1) * NZ + z


def shift(dx=0, dy=0, dz=0):
    pairs = []
    for source in range(2 * NX * NY * NZ):
        x, y, z, core = split(source)
        pairs.append((source, join(x + dx, y + dy, z + dz, core)))
    return pairs


def spread():
    pairs = []
    for source in range(2 * NX * NY * NZ):
        x, y, z, core = split(source)
        col = (y >> 1) * NZ + z
        row, half = col // 2, col % 2
        place = PLACES[row][4 * (4 * half + x) + 2 * (y & 1) + core]
        pairs.append((source, row * 2 * NZ + place))
    return pairs


def send(block, pairs):
    return lax.ppermute(block, JOINT, pairs)


def dequantize_body(mantissa_ref, exponent_ref, out, mantissa, exponent, sems):
    first = pltpu.make_async_copy(mantissa_ref, mantissa, sems.at[0])
    second = pltpu.make_async_copy(exponent_ref, exponent, sems.at[1])
    first.start()
    second.start()
    second.wait()
    scale = jnp.exp2(exponent[...].astype(jnp.float32)).T
    first.wait()
    for k in range(DEPTH // 128):
        span = slice(128 * k, 128 * (k + 1))
        out[:, span] = (mantissa[:, span].astype(jnp.float32) * scale[:, k : k + 1]).astype(jnp.bfloat16)


def dequantize(mantissa, exponent):
    anywhere = pl.BlockSpec(memory_space=pltpu.HBM)
    return pl.pallas_call(
        dequantize_body,
        out_shape=jax.ShapeDtypeStruct(mantissa.shape, jnp.bfloat16),
        in_specs=[anywhere, anywhere],
        out_specs=pl.BlockSpec(memory_space=pltpu.VMEM),
        scratch_shapes=[
            pltpu.VMEM(mantissa.shape, mantissa.dtype),
            pltpu.VMEM(exponent.shape[::-1], exponent.dtype),
            pltpu.SemaphoreType.DMA((2,)),
        ],
        compiler_params=pltpu.CompilerParams(vmem_limit_bytes=LIMIT),
    )(mantissa, exponent.T)


def scale_body(weights, rows, out):
    for k in range(DEPTH // 256):
        span = slice(256 * k, 256 * (k + 1))
        out[span, :] = (rows[:, span].astype(jnp.float32) * weights[:, span]).astype(jnp.bfloat16).T


def scale(weights, rows):
    whole = pl.BlockSpec(memory_space=pltpu.VMEM)
    return pl.pallas_call(
        scale_body,
        out_shape=jax.ShapeDtypeStruct((DEPTH, COLS), jnp.bfloat16),
        in_specs=[whole, whole],
        out_specs=whole,
        compiler_params=pltpu.CompilerParams(vmem_limit_bytes=LIMIT),
        cost_estimate=pl.CostEstimate(flops=COLS, bytes_accessed=COLS, transcendentals=0),
    )(weights, rows)


def multiply_body(first, order, columns, *rest):
    *blocks, response, held, sems = rest
    copies = []
    for block in blocks:
        for k in range(block.shape[0] // ROWS):
            slot = len(copies)
            held[slot] = jnp.dot(
                block[ROWS * k : ROWS * (k + 1), :], columns[...], preferred_element_type=jnp.float32
            )
            copies.append(pltpu.make_async_copy(held.at[slot], response.at[order[first + slot]], sems.at[slot]))
            copies[-1].start()
    for copy in copies:
        copy.wait()


def multiply(first, order, columns, blocks, response):
    count = sum(block.shape[0] for block in blocks) // ROWS
    whole = pl.BlockSpec(memory_space=pltpu.VMEM)
    anywhere = pl.BlockSpec(memory_space=pl.ANY)
    in_specs = [pl.BlockSpec(memory_space=pltpu.SMEM)] + [whole] * (1 + len(blocks))
    args = [order, columns, *blocks]
    aliases = {}

    def body(*refs):
        if response is not None:
            refs = refs[: len(args) - 1] + refs[len(args) :]
        multiply_body(first, *refs)

    if response is not None:
        in_specs.append(anywhere)
        args.append(response)
        aliases = {len(args) - 1: 0}
    return pl.pallas_call(
        body,
        out_shape=jax.ShapeDtypeStruct((CHUNKS, ROWS, COLS), jnp.float32),
        in_specs=in_specs,
        out_specs=anywhere,
        scratch_shapes=[pltpu.VMEM((count, ROWS, COLS), jnp.float32), pltpu.SemaphoreType.DMA((count,))],
        input_output_aliases=aliases,
        compiler_params=pltpu.CompilerParams(vmem_limit_bytes=LIMIT),
        cost_estimate=pl.CostEstimate(flops=count * ROWS, bytes_accessed=count * ROWS, transcendentals=0),
    )(*args)


def pair_weights(occ_level, virt_level):
    energy_gap = 0.01 * (virt_level - occ_level).astype(jnp.float32)
    return -4.0 * energy_gap / (energy_gap * energy_gap + 1.0)


def per_device(mantissa, exponent, occ_level, virt_level):
    row, col = lax.axis_index("prow"), lax.axis_index("pcol")

    own = dequantize(mantissa, exponent)
    same_x = [[4 * x + i for i in range(4)] for x in range(NX)]
    group = lax.all_gather(own, "prow", axis=0, tiled=True, axis_index_groups=same_x)

    placed = send(group, spread())
    along_x = [[4 * x + i for x in range(NX)] for i in range(4)]
    groups = lax.all_to_all(
        jnp.broadcast_to(group, (NX, *group.shape)), "prow", 0, 0, axis_index_groups=along_x
    )
    down = send(placed, shift(dz=1))
    up = send(placed, shift(dz=-1))
    over = send(placed, shift(dy=2))
    weights = pair_weights(occ_level, virt_level)[None, :]
    columns = scale(weights, groups.reshape(COLS, DEPTH))
    steps = jnp.array([0, 7, 1, 4, 6, 2, 3, 5], jnp.int32)
    order = jnp.take(jnp.asarray(chunk_table()), row * CHUNKS + (color_of(row, col) + steps) % CHUNKS)
    down, up, over, order = lax.optimization_barrier((down, up, over, order))
    sides = jnp.concatenate([down, up], axis=0)
    over_sides = send(sides, shift(dy=2))
    down_two = send(down, shift(dz=1))
    up_two = send(up, shift(dz=-1))

    response = multiply(0, order, columns, [placed, down, up, over], None)
    response = multiply(4, order, columns, [down_two, up_two, over_sides], response)
    return response.reshape(CHUNKS * ROWS, COLS)


def solution(mesh):
    return jax.shard_map(
        per_device,
        mesh=mesh,
        in_specs=(P(("pcol", "prow"), None), P(("pcol", "prow"), None), P(), P()),
        out_specs=P("prow", "pcol"),
        check_vma=False,
    )
```

```python
import jax
import jax.numpy as jnp
import numpy as np
from jax import lax
from jax.experimental import pallas as pl
from jax.experimental.pallas import tpu as pltpu
from jax.sharding import PartitionSpec as P

NX, NY, NZ = 4, 4, 16
ROWS = 160
CHUNKS = 8
DEPTH = 1024
COLS = 640
JOINT = ("prow", "pcol")
LIMIT = 32 * 1024 * 1024

PLACES = (
    (6, 14, 26, 18, 9, 1, 21, 29, 5, 13, 25, 17, 2, 10, 22, 30, 12, 4, 24, 16, 0, 8, 28, 20, 3, 11, 23, 31, 15, 7, 19, 27),
    (15, 7, 19, 27, 3, 11, 23, 31, 0, 8, 28, 20, 4, 12, 16, 24, 13, 5, 25, 17, 10, 2, 22, 30, 6, 14, 26, 18, 1, 9, 21, 29),
    (17, 25, 13, 5, 30, 22, 2, 10, 26, 18, 14, 6, 21, 29, 1, 9, 24, 16, 4, 12, 28, 20, 0, 8, 19, 27, 15, 7, 23, 31, 3, 11),
    (19, 27, 7, 15, 23, 31, 11, 3, 16, 24, 4, 12, 28, 20, 8, 0, 30, 22, 10, 2, 21, 29, 9, 1, 25, 17, 5, 13, 26, 18, 6, 14),
    (2, 10, 30, 22, 1, 9, 29, 21, 5, 13, 25, 17, 6, 14, 26, 18, 4, 12, 16, 24, 8, 0, 20, 28, 11, 3, 23, 31, 15, 7, 27, 19),
    (15, 7, 27, 19, 11, 3, 23, 31, 0, 8, 20, 28, 4, 12, 16, 24, 13, 5, 25, 17, 2, 10, 30, 22, 14, 6, 26, 18, 1, 9, 29, 21),
    (18, 26, 14, 6, 22, 30, 10, 2, 17, 25, 13, 5, 29, 21, 1, 9, 16, 24, 12, 4, 28, 20, 0, 8, 31, 23, 3, 11, 27, 19, 15, 7),
    (19, 27, 15, 7, 31, 23, 11, 3, 28, 20, 8, 0, 24, 16, 12, 4, 17, 25, 13, 5, 21, 29, 1, 9, 26, 18, 14, 6, 22, 30, 2, 10),
    (18, 26, 14, 6, 29, 21, 1, 9, 22, 30, 10, 2, 25, 17, 5, 13, 31, 23, 11, 3, 19, 27, 7, 15, 16, 24, 12, 4, 20, 28, 0, 8),
    (28, 20, 8, 0, 24, 16, 12, 4, 19, 27, 7, 15, 23, 31, 11, 3, 30, 22, 10, 2, 17, 25, 5, 13, 29, 21, 1, 9, 18, 26, 6, 14),
    (1, 9, 29, 21, 6, 14, 18, 26, 2, 10, 22, 30, 13, 5, 25, 17, 0, 8, 20, 28, 4, 12, 24, 16, 7, 15, 19, 27, 3, 11, 31, 23),
    (3, 11, 23, 31, 15, 7, 19, 27, 4, 12, 24, 16, 0, 8, 28, 20, 5, 13, 17, 25, 2, 10, 30, 22, 9, 1, 29, 21, 14, 6, 26, 18),
    (17, 25, 13, 5, 29, 21, 9, 1, 30, 22, 2, 10, 18, 26, 14, 6, 28, 20, 0, 8, 24, 16, 4, 12, 19, 27, 15, 7, 23, 31, 11, 3),
    (31, 23, 11, 3, 27, 19, 7, 15, 16, 24, 12, 4, 28, 20, 0, 8, 26, 18, 14, 6, 22, 30, 2, 10, 21, 29, 9, 1, 25, 17, 5, 13),
    (14, 6, 26, 18, 9, 1, 29, 21, 2, 10, 22, 30, 13, 5, 25, 17, 0, 8, 20, 28, 4, 12, 24, 16, 15, 7, 27, 19, 11, 3, 31, 23),
    (11, 3, 31, 23, 15, 7, 19, 27, 12, 4, 24, 16, 8, 0, 28, 20, 13, 5, 25, 17, 10, 2, 30, 22, 9, 1, 21, 29, 14, 6, 26, 18),
)


def color_of(row, col):
    return (col % NZ + 4 * (col // NZ) - 2 * row) % CHUNKS


def chunk_table():
    table = np.zeros((16, CHUNKS), np.int32)
    for row, places in enumerate(PLACES):
        for slot, col in enumerate(places):
            table[row, color_of(row, col)] = slot // 4
    return table


def split(index):
    row, col = divmod(index, 2 * NZ)
    return row >> 2, (col // NZ) * 2 + ((row >> 1) & 1), col % NZ, row & 1


def join(x, y, z, core):
    x, y, z = x % NX, y % NY, z % NZ
    return (x * 4 + (y & 1) * 2 + core) * 2 * NZ + (y >> 1) * NZ + z


def shift(dx=0, dy=0, dz=0):
    pairs = []
    for source in range(2 * NX * NY * NZ):
        x, y, z, core = split(source)
        pairs.append((source, join(x + dx, y + dy, z + dz, core)))
    return pairs


def spread():
    pairs = []
    for source in range(2 * NX * NY * NZ):
        x, y, z, core = split(source)
        col = (y >> 1) * NZ + z
        row, half = col // 2, col % 2
        place = PLACES[row][4 * (4 * half + x) + 2 * (y & 1) + core]
        pairs.append((source, row * 2 * NZ + place))
    return pairs


def send(block, pairs):
    return lax.ppermute(block, JOINT, pairs)


def dequantize_body(mantissa_ref, exponent_ref, out, mantissa, exponent, sems):
    first = pltpu.make_async_copy(mantissa_ref, mantissa, sems.at[0])
    second = pltpu.make_async_copy(exponent_ref, exponent, sems.at[1])
    first.start()
    second.start()
    second.wait()
    scale = jnp.exp2(exponent[...].astype(jnp.float32)).T
    first.wait()
    for k in range(DEPTH // 128):
        span = slice(128 * k, 128 * (k + 1))
        out[:, span] = (mantissa[:, span].astype(jnp.float32) * scale[:, k : k + 1]).astype(jnp.bfloat16)


def dequantize(mantissa, exponent):
    anywhere = pl.BlockSpec(memory_space=pltpu.HBM)
    return pl.pallas_call(
        dequantize_body,
        out_shape=jax.ShapeDtypeStruct(mantissa.shape, jnp.bfloat16),
        in_specs=[anywhere, anywhere],
        out_specs=pl.BlockSpec(memory_space=pltpu.VMEM),
        scratch_shapes=[
            pltpu.VMEM(mantissa.shape, mantissa.dtype),
            pltpu.VMEM(exponent.shape[::-1], exponent.dtype),
            pltpu.SemaphoreType.DMA((2,)),
        ],
        compiler_params=pltpu.CompilerParams(vmem_limit_bytes=LIMIT),
    )(mantissa, exponent.T)


def scale_body(weights, rows, out):
    for k in range(DEPTH // 256):
        span = slice(256 * k, 256 * (k + 1))
        out[span, :] = (rows[:, span].astype(jnp.float32) * weights[:, span]).astype(jnp.bfloat16).T


def scale(weights, rows):
    whole = pl.BlockSpec(memory_space=pltpu.VMEM)
    return pl.pallas_call(
        scale_body,
        out_shape=jax.ShapeDtypeStruct((DEPTH, COLS), jnp.bfloat16),
        in_specs=[whole, whole],
        out_specs=whole,
        compiler_params=pltpu.CompilerParams(vmem_limit_bytes=LIMIT),
        cost_estimate=pl.CostEstimate(flops=COLS, bytes_accessed=COLS, transcendentals=0),
    )(weights, rows)


def stack_body(first, second, out):
    out[:ROWS, :] = first[...]
    out[ROWS:, :] = second[...]


def stack(first, second):
    whole = pl.BlockSpec(memory_space=pltpu.VMEM)
    return pl.pallas_call(
        stack_body,
        out_shape=jax.ShapeDtypeStruct((2 * ROWS, DEPTH), jnp.bfloat16),
        in_specs=[whole, whole],
        out_specs=whole,
        compiler_params=pltpu.CompilerParams(vmem_limit_bytes=LIMIT),
        cost_estimate=pl.CostEstimate(flops=ROWS, bytes_accessed=ROWS, transcendentals=0),
    )(first, second)


def multiply_body(first, order, columns, *rest):
    *blocks, response, held, sems = rest
    copies = []
    for block in blocks:
        for k in range(block.shape[0] // ROWS):
            slot = len(copies)
            held[slot] = jnp.dot(
                block[ROWS * k : ROWS * (k + 1), :], columns[...], preferred_element_type=jnp.float32
            )
            copies.append(pltpu.make_async_copy(held.at[slot], response.at[order[first + slot]], sems.at[slot]))
            copies[-1].start()
    for copy in copies:
        copy.wait()


def multiply(first, order, columns, blocks, response):
    count = sum(block.shape[0] for block in blocks) // ROWS
    whole = pl.BlockSpec(memory_space=pltpu.VMEM)
    anywhere = pl.BlockSpec(memory_space=pl.ANY)
    in_specs = [pl.BlockSpec(memory_space=pltpu.SMEM)] + [whole] * (1 + len(blocks))
    args = [order, columns, *blocks]
    aliases = {}

    def body(*refs):
        if response is not None:
            refs = refs[: len(args) - 1] + refs[len(args) :]
        multiply_body(first, *refs)

    if response is not None:
        in_specs.append(anywhere)
        args.append(response)
        aliases = {len(args) - 1: 0}
    return pl.pallas_call(
        body,
        out_shape=jax.ShapeDtypeStruct((CHUNKS, ROWS, COLS), jnp.float32),
        in_specs=in_specs,
        out_specs=anywhere,
        scratch_shapes=[pltpu.VMEM((count, ROWS, COLS), jnp.float32), pltpu.SemaphoreType.DMA((count,))],
        input_output_aliases=aliases,
        compiler_params=pltpu.CompilerParams(vmem_limit_bytes=LIMIT),
        cost_estimate=pl.CostEstimate(flops=count * ROWS, bytes_accessed=count * ROWS, transcendentals=0),
    )(*args)


def pair_weights(occ_level, virt_level):
    energy_gap = 0.01 * (virt_level - occ_level).astype(jnp.float32)
    return -4.0 * energy_gap / (energy_gap * energy_gap + 1.0)


def per_device(mantissa, exponent, occ_level, virt_level):
    row, col = lax.axis_index("prow"), lax.axis_index("pcol")

    own = dequantize(mantissa, exponent)
    same_x = [[4 * x + i for i in range(4)] for x in range(NX)]
    group = lax.all_gather(own, "prow", axis=0, tiled=True, axis_index_groups=same_x)

    placed = send(group, spread())
    along_x = [[4 * x + i for x in range(NX)] for i in range(4)]
    groups = lax.all_to_all(
        jnp.broadcast_to(group, (NX, *group.shape)), "prow", 0, 0, axis_index_groups=along_x
    )
    down = send(placed, shift(dz=1))
    up = send(placed, shift(dz=-1))
    over = send(placed, shift(dy=2))
    weights = pair_weights(occ_level, virt_level)[None, :]
    columns = scale(weights, groups.reshape(COLS, DEPTH))
    steps = jnp.array([0, 7, 1, 4, 6, 2, 3, 5], jnp.int32)
    order = jnp.take(jnp.asarray(chunk_table()), row * CHUNKS + (color_of(row, col) + steps) % CHUNKS)
    down, up, over, order = lax.optimization_barrier((down, up, over, order))
    sides = stack(down, up)
    over_sides = send(sides, shift(dy=2))
    down_two = send(down, shift(dz=1))
    up_two = send(up, shift(dz=-1))

    response = multiply(0, order, columns, [placed, down, up, over], None)
    response = multiply(4, order, columns, [down_two, up_two], response)
    response = multiply(6, order, columns, [over_sides], response)
    return response.reshape(CHUNKS * ROWS, COLS)


def solution(mesh):
    return jax.shard_map(
        per_device,
        mesh=mesh,
        in_specs=(P(("pcol", "prow"), None), P(("pcol", "prow"), None), P(), P()),
        out_specs=P("prow", "pcol"),
        check_vma=False,
    )
```

```python
import jax
import jax.numpy as jnp
import numpy as np
from jax import lax
from jax.experimental import pallas as pl
from jax.experimental.pallas import tpu as pltpu
from jax.sharding import PartitionSpec as P

NX, NY, NZ = 4, 4, 16
ROWS = 160
CHUNKS = 8
DEPTH = 1024
COLS = 640
JOINT = ("prow", "pcol")
LIMIT = 32 * 1024 * 1024

PLACES = (
    (6, 14, 26, 18, 9, 1, 21, 29, 5, 13, 25, 17, 2, 10, 22, 30, 12, 4, 24, 16, 0, 8, 28, 20, 3, 11, 23, 31, 15, 7, 19, 27),
    (15, 7, 19, 27, 3, 11, 23, 31, 0, 8, 28, 20, 4, 12, 16, 24, 13, 5, 25, 17, 10, 2, 22, 30, 6, 14, 26, 18, 1, 9, 21, 29),
    (17, 25, 13, 5, 30, 22, 2, 10, 26, 18, 14, 6, 21, 29, 1, 9, 24, 16, 4, 12, 28, 20, 0, 8, 19, 27, 15, 7, 23, 31, 3, 11),
    (19, 27, 7, 15, 23, 31, 11, 3, 16, 24, 4, 12, 28, 20, 8, 0, 30, 22, 10, 2, 21, 29, 9, 1, 25, 17, 5, 13, 26, 18, 6, 14),
    (2, 10, 30, 22, 1, 9, 29, 21, 5, 13, 25, 17, 6, 14, 26, 18, 4, 12, 16, 24, 8, 0, 20, 28, 11, 3, 23, 31, 15, 7, 27, 19),
    (15, 7, 27, 19, 11, 3, 23, 31, 0, 8, 20, 28, 4, 12, 16, 24, 13, 5, 25, 17, 2, 10, 30, 22, 14, 6, 26, 18, 1, 9, 29, 21),
    (18, 26, 14, 6, 22, 30, 10, 2, 17, 25, 13, 5, 29, 21, 1, 9, 16, 24, 12, 4, 28, 20, 0, 8, 31, 23, 3, 11, 27, 19, 15, 7),
    (19, 27, 15, 7, 31, 23, 11, 3, 28, 20, 8, 0, 24, 16, 12, 4, 17, 25, 13, 5, 21, 29, 1, 9, 26, 18, 14, 6, 22, 30, 2, 10),
    (18, 26, 14, 6, 29, 21, 1, 9, 22, 30, 10, 2, 25, 17, 5, 13, 31, 23, 11, 3, 19, 27, 7, 15, 16, 24, 12, 4, 20, 28, 0, 8),
    (28, 20, 8, 0, 24, 16, 12, 4, 19, 27, 7, 15, 23, 31, 11, 3, 30, 22, 10, 2, 17, 25, 5, 13, 29, 21, 1, 9, 18, 26, 6, 14),
    (1, 9, 29, 21, 6, 14, 18, 26, 2, 10, 22, 30, 13, 5, 25, 17, 0, 8, 20, 28, 4, 12, 24, 16, 7, 15, 19, 27, 3, 11, 31, 23),
    (3, 11, 23, 31, 15, 7, 19, 27, 4, 12, 24, 16, 0, 8, 28, 20, 5, 13, 17, 25, 2, 10, 30, 22, 9, 1, 29, 21, 14, 6, 26, 18),
    (17, 25, 13, 5, 29, 21, 9, 1, 30, 22, 2, 10, 18, 26, 14, 6, 28, 20, 0, 8, 24, 16, 4, 12, 19, 27, 15, 7, 23, 31, 11, 3),
    (31, 23, 11, 3, 27, 19, 7, 15, 16, 24, 12, 4, 28, 20, 0, 8, 26, 18, 14, 6, 22, 30, 2, 10, 21, 29, 9, 1, 25, 17, 5, 13),
    (14, 6, 26, 18, 9, 1, 29, 21, 2, 10, 22, 30, 13, 5, 25, 17, 0, 8, 20, 28, 4, 12, 24, 16, 15, 7, 27, 19, 11, 3, 31, 23),
    (11, 3, 31, 23, 15, 7, 19, 27, 12, 4, 24, 16, 8, 0, 28, 20, 13, 5, 25, 17, 10, 2, 30, 22, 9, 1, 21, 29, 14, 6, 26, 18),
)


def color_of(row, col):
    return (col % NZ + 4 * (col // NZ) - 2 * row) % CHUNKS


def chunk_table():
    table = np.zeros((16, CHUNKS), np.int32)
    for row, places in enumerate(PLACES):
        for slot, col in enumerate(places):
            table[row, color_of(row, col)] = slot // 4
    return table


def split(index):
    row, col = divmod(index, 2 * NZ)
    return row >> 2, (col // NZ) * 2 + ((row >> 1) & 1), col % NZ, row & 1


def join(x, y, z, core):
    x, y, z = x % NX, y % NY, z % NZ
    return (x * 4 + (y & 1) * 2 + core) * 2 * NZ + (y >> 1) * NZ + z


def shift(dx=0, dy=0, dz=0):
    pairs = []
    for source in range(2 * NX * NY * NZ):
        x, y, z, core = split(source)
        pairs.append((source, join(x + dx, y + dy, z + dz, core)))
    return pairs


def spread():
    pairs = []
    for source in range(2 * NX * NY * NZ):
        x, y, z, core = split(source)
        col = (y >> 1) * NZ + z
        row, half = col // 2, col % 2
        place = PLACES[row][4 * (4 * half + x) + 2 * (y & 1) + core]
        pairs.append((source, row * 2 * NZ + place))
    return pairs


def send(block, pairs):
    return lax.ppermute(block, JOINT, pairs)


def dequantize_body(mantissa_ref, exponent_ref, out, mantissa, exponent, sems):
    first = pltpu.make_async_copy(mantissa_ref, mantissa, sems.at[0])
    second = pltpu.make_async_copy(exponent_ref, exponent, sems.at[1])
    first.start()
    second.start()
    second.wait()
    scale = jnp.exp2(exponent[...].astype(jnp.float32)).T
    first.wait()
    for k in range(DEPTH // 128):
        span = slice(128 * k, 128 * (k + 1))
        out[:, span] = (mantissa[:, span].astype(jnp.float32) * scale[:, k : k + 1]).astype(jnp.bfloat16)


def dequantize(mantissa, exponent):
    anywhere = pl.BlockSpec(memory_space=pltpu.HBM)
    return pl.pallas_call(
        dequantize_body,
        out_shape=jax.ShapeDtypeStruct(mantissa.shape, jnp.bfloat16),
        in_specs=[anywhere, anywhere],
        out_specs=pl.BlockSpec(memory_space=pltpu.VMEM),
        scratch_shapes=[
            pltpu.VMEM(mantissa.shape, mantissa.dtype),
            pltpu.VMEM(exponent.shape[::-1], exponent.dtype),
            pltpu.SemaphoreType.DMA((2,)),
        ],
        compiler_params=pltpu.CompilerParams(vmem_limit_bytes=LIMIT),
    )(mantissa, exponent.T)


def scale_body(weights, rows, out):
    for k in range(DEPTH // 256):
        span = slice(256 * k, 256 * (k + 1))
        out[span, :] = (rows[:, span].astype(jnp.float32) * weights[:, span]).astype(jnp.bfloat16).T


def scale(weights, rows):
    whole = pl.BlockSpec(memory_space=pltpu.VMEM)
    return pl.pallas_call(
        scale_body,
        out_shape=jax.ShapeDtypeStruct((DEPTH, COLS), jnp.bfloat16),
        in_specs=[whole, whole],
        out_specs=whole,
        compiler_params=pltpu.CompilerParams(vmem_limit_bytes=LIMIT),
        cost_estimate=pl.CostEstimate(flops=COLS, bytes_accessed=COLS, transcendentals=0),
    )(weights, rows)


def multiply_body(first, order, columns, *rest):
    *blocks, response, held, sems = rest
    copies = []
    for block in blocks:
        for k in range(block.shape[0] // ROWS):
            slot = len(copies)
            held[slot] = jnp.dot(
                block[ROWS * k : ROWS * (k + 1), :], columns[...], preferred_element_type=jnp.float32
            )
            copies.append(pltpu.make_async_copy(held.at[slot], response.at[order[first + slot]], sems.at[slot]))
            copies[-1].start()
    for copy in copies:
        copy.wait()


def multiply(first, order, columns, blocks, response):
    count = sum(block.shape[0] for block in blocks) // ROWS
    whole = pl.BlockSpec(memory_space=pltpu.VMEM)
    anywhere = pl.BlockSpec(memory_space=pl.ANY)
    in_specs = [pl.BlockSpec(memory_space=pltpu.SMEM)] + [whole] * (1 + len(blocks))
    args = [order, columns, *blocks]
    aliases = {}

    def body(*refs):
        if response is not None:
            refs = refs[: len(args) - 1] + refs[len(args) :]
        multiply_body(first, *refs)

    if response is not None:
        in_specs.append(anywhere)
        args.append(response)
        aliases = {len(args) - 1: 0}
    return pl.pallas_call(
        body,
        out_shape=jax.ShapeDtypeStruct((CHUNKS, ROWS, COLS), jnp.float32),
        in_specs=in_specs,
        out_specs=anywhere,
        scratch_shapes=[pltpu.VMEM((count, ROWS, COLS), jnp.float32), pltpu.SemaphoreType.DMA((count,))],
        input_output_aliases=aliases,
        compiler_params=pltpu.CompilerParams(vmem_limit_bytes=LIMIT),
        cost_estimate=pl.CostEstimate(flops=count * ROWS, bytes_accessed=count * ROWS, transcendentals=0),
    )(*args)


def pair_weights(occ_level, virt_level):
    energy_gap = 0.01 * (virt_level - occ_level).astype(jnp.float32)
    return -4.0 * energy_gap / (energy_gap * energy_gap + 1.0)


def per_device(mantissa, exponent, occ_level, virt_level):
    row, col = lax.axis_index("prow"), lax.axis_index("pcol")

    own = dequantize(mantissa, exponent)
    same_x = [[4 * x + i for i in range(4)] for x in range(NX)]
    group = lax.all_gather(own, "prow", axis=0, tiled=True, axis_index_groups=same_x)

    placed = send(group, spread())
    along_x = [[4 * x + i for x in range(NX)] for i in range(4)]
    groups = lax.all_to_all(
        jnp.broadcast_to(group, (NX, *group.shape)), "prow", 0, 0, axis_index_groups=along_x
    )
    down = send(placed, shift(dz=1))
    up = send(placed, shift(dz=-1))
    over = send(placed, shift(dy=2))
    weights = pair_weights(occ_level, virt_level)[None, :]
    columns = scale(weights, groups.reshape(COLS, DEPTH))
    steps = jnp.array([0, 1, 4, 7, 2, 5, 6, 3], jnp.int32)
    order = jnp.take(jnp.asarray(chunk_table()), row * CHUNKS + (color_of(row, col) + steps) % CHUNKS)
    over_up = send(up, shift(dy=2))
    over_down = send(down, shift(dy=2))
    up_two = send(up, shift(dz=-1))
    down_two = send(down, shift(dz=1))

    response = multiply(0, order, columns, [placed, up, over], None)
    response = multiply(3, order, columns, [down], response)
    response = multiply(4, order, columns, [up_two, over_up], response)
    response = multiply(6, order, columns, [down_two, over_down], response)
    return response.reshape(CHUNKS * ROWS, COLS)


def solution(mesh):
    return jax.shard_map(
        per_device,
        mesh=mesh,
        in_specs=(P(("pcol", "prow"), None), P(("pcol", "prow"), None), P(), P()),
        out_specs=P("prow", "pcol"),
        check_vma=False,
    )
```

```python
import jax
import jax.numpy as jnp
import numpy as np
from jax import lax
from jax.experimental import pallas as pl
from jax.experimental.pallas import tpu as pltpu
from jax.sharding import PartitionSpec as P

NX, NY, NZ = 4, 4, 16
ROWS = 160
CHUNKS = 8
DEPTH = 1024
COLS = 640
JOINT = ("prow", "pcol")
LIMIT = 32 * 1024 * 1024

PLACES = (
    (6, 14, 26, 18, 9, 1, 21, 29, 5, 13, 25, 17, 2, 10, 22, 30, 12, 4, 24, 16, 0, 8, 28, 20, 3, 11, 23, 31, 15, 7, 19, 27),
    (15, 7, 19, 27, 3, 11, 23, 31, 0, 8, 28, 20, 4, 12, 16, 24, 13, 5, 25, 17, 10, 2, 22, 30, 6, 14, 26, 18, 1, 9, 21, 29),
    (17, 25, 13, 5, 30, 22, 2, 10, 26, 18, 14, 6, 21, 29, 1, 9, 24, 16, 4, 12, 28, 20, 0, 8, 19, 27, 15, 7, 23, 31, 3, 11),
    (19, 27, 7, 15, 23, 31, 11, 3, 16, 24, 4, 12, 28, 20, 8, 0, 30, 22, 10, 2, 21, 29, 9, 1, 25, 17, 5, 13, 26, 18, 6, 14),
    (2, 10, 30, 22, 1, 9, 29, 21, 5, 13, 25, 17, 6, 14, 26, 18, 4, 12, 16, 24, 8, 0, 20, 28, 11, 3, 23, 31, 15, 7, 27, 19),
    (15, 7, 27, 19, 11, 3, 23, 31, 0, 8, 20, 28, 4, 12, 16, 24, 13, 5, 25, 17, 2, 10, 30, 22, 14, 6, 26, 18, 1, 9, 29, 21),
    (18, 26, 14, 6, 22, 30, 10, 2, 17, 25, 13, 5, 29, 21, 1, 9, 16, 24, 12, 4, 28, 20, 0, 8, 31, 23, 3, 11, 27, 19, 15, 7),
    (19, 27, 15, 7, 31, 23, 11, 3, 28, 20, 8, 0, 24, 16, 12, 4, 17, 25, 13, 5, 21, 29, 1, 9, 26, 18, 14, 6, 22, 30, 2, 10),
    (18, 26, 14, 6, 29, 21, 1, 9, 22, 30, 10, 2, 25, 17, 5, 13, 31, 23, 11, 3, 19, 27, 7, 15, 16, 24, 12, 4, 20, 28, 0, 8),
    (28, 20, 8, 0, 24, 16, 12, 4, 19, 27, 7, 15, 23, 31, 11, 3, 30, 22, 10, 2, 17, 25, 5, 13, 29, 21, 1, 9, 18, 26, 6, 14),
    (1, 9, 29, 21, 6, 14, 18, 26, 2, 10, 22, 30, 13, 5, 25, 17, 0, 8, 20, 28, 4, 12, 24, 16, 7, 15, 19, 27, 3, 11, 31, 23),
    (3, 11, 23, 31, 15, 7, 19, 27, 4, 12, 24, 16, 0, 8, 28, 20, 5, 13, 17, 25, 2, 10, 30, 22, 9, 1, 29, 21, 14, 6, 26, 18),
    (17, 25, 13, 5, 29, 21, 9, 1, 30, 22, 2, 10, 18, 26, 14, 6, 28, 20, 0, 8, 24, 16, 4, 12, 19, 27, 15, 7, 23, 31, 11, 3),
    (31, 23, 11, 3, 27, 19, 7, 15, 16, 24, 12, 4, 28, 20, 0, 8, 26, 18, 14, 6, 22, 30, 2, 10, 21, 29, 9, 1, 25, 17, 5, 13),
    (14, 6, 26, 18, 9, 1, 29, 21, 2, 10, 22, 30, 13, 5, 25, 17, 0, 8, 20, 28, 4, 12, 24, 16, 15, 7, 27, 19, 11, 3, 31, 23),
    (11, 3, 31, 23, 15, 7, 19, 27, 12, 4, 24, 16, 8, 0, 28, 20, 13, 5, 25, 17, 10, 2, 30, 22, 9, 1, 21, 29, 14, 6, 26, 18),
)


def color_of(row, col):
    return (col % NZ + 4 * (col // NZ) - 2 * row) % CHUNKS


def chunk_table():
    table = np.zeros((16, CHUNKS), np.int32)
    for row, places in enumerate(PLACES):
        for slot, col in enumerate(places):
            table[row, color_of(row, col)] = slot // 4
    return table


def split(index):
    row, col = divmod(index, 2 * NZ)
    return row >> 2, (col // NZ) * 2 + ((row >> 1) & 1), col % NZ, row & 1


def join(x, y, z, core):
    x, y, z = x % NX, y % NY, z % NZ
    return (x * 4 + (y & 1) * 2 + core) * 2 * NZ + (y >> 1) * NZ + z


def shift(dx=0, dy=0, dz=0):
    pairs = []
    for source in range(2 * NX * NY * NZ):
        x, y, z, core = split(source)
        pairs.append((source, join(x + dx, y + dy, z + dz, core)))
    return pairs


def spread():
    pairs = []
    for source in range(2 * NX * NY * NZ):
        x, y, z, core = split(source)
        col = (y >> 1) * NZ + z
        row, half = col // 2, col % 2
        place = PLACES[row][4 * (4 * half + x) + 2 * (y & 1) + core]
        pairs.append((source, row * 2 * NZ + place))
    return pairs


def send(block, pairs):
    return lax.ppermute(block, JOINT, pairs)


def dequantize_body(mantissa_ref, exponent_ref, out, mantissa, exponent, sems):
    first = pltpu.make_async_copy(mantissa_ref, mantissa, sems.at[0])
    second = pltpu.make_async_copy(exponent_ref, exponent, sems.at[1])
    first.start()
    second.start()
    second.wait()
    scale = jnp.exp2(exponent[...].astype(jnp.float32)).T
    first.wait()
    for k in range(DEPTH // 128):
        span = slice(128 * k, 128 * (k + 1))
        out[:, span] = (mantissa[:, span].astype(jnp.float32) * scale[:, k : k + 1]).astype(jnp.bfloat16)


def dequantize(mantissa, exponent):
    anywhere = pl.BlockSpec(memory_space=pltpu.HBM)
    return pl.pallas_call(
        dequantize_body,
        out_shape=jax.ShapeDtypeStruct(mantissa.shape, jnp.bfloat16),
        in_specs=[anywhere, anywhere],
        out_specs=pl.BlockSpec(memory_space=pltpu.VMEM),
        scratch_shapes=[
            pltpu.VMEM(mantissa.shape, mantissa.dtype),
            pltpu.VMEM(exponent.shape[::-1], exponent.dtype),
            pltpu.SemaphoreType.DMA((2,)),
        ],
        compiler_params=pltpu.CompilerParams(vmem_limit_bytes=LIMIT),
    )(mantissa, exponent.T)


def scale_body(weights, rows, out):
    for k in range(DEPTH // 256):
        span = slice(256 * k, 256 * (k + 1))
        out[span, :] = (rows[:, span].astype(jnp.float32) * weights[:, span]).astype(jnp.bfloat16).T


def scale(weights, rows):
    whole = pl.BlockSpec(memory_space=pltpu.VMEM)
    return pl.pallas_call(
        scale_body,
        out_shape=jax.ShapeDtypeStruct((DEPTH, COLS), jnp.bfloat16),
        in_specs=[whole, whole],
        out_specs=whole,
        compiler_params=pltpu.CompilerParams(vmem_limit_bytes=LIMIT),
        cost_estimate=pl.CostEstimate(flops=COLS, bytes_accessed=COLS, transcendentals=0),
    )(weights, rows)


def multiply_body(first, order, columns, *rest):
    *blocks, response, held, sems = rest
    copies = []
    for block in blocks:
        for k in range(block.shape[0] // ROWS):
            slot = len(copies)
            held[slot] = jnp.dot(
                block[ROWS * k : ROWS * (k + 1), :], columns[...], preferred_element_type=jnp.float32
            )
            copies.append(pltpu.make_async_copy(held.at[slot], response.at[order[first + slot]], sems.at[slot]))
            copies[-1].start()
    for copy in copies:
        copy.wait()


def multiply(first, order, columns, blocks, response):
    count = sum(block.shape[0] for block in blocks) // ROWS
    whole = pl.BlockSpec(memory_space=pltpu.VMEM)
    anywhere = pl.BlockSpec(memory_space=pl.ANY)
    in_specs = [pl.BlockSpec(memory_space=pltpu.SMEM)] + [whole] * (1 + len(blocks))
    args = [order, columns, *blocks]
    aliases = {}

    def body(*refs):
        if response is not None:
            refs = refs[: len(args) - 1] + refs[len(args) :]
        multiply_body(first, *refs)

    if response is not None:
        in_specs.append(anywhere)
        args.append(response)
        aliases = {len(args) - 1: 0}
    return pl.pallas_call(
        body,
        out_shape=jax.ShapeDtypeStruct((CHUNKS, ROWS, COLS), jnp.float32),
        in_specs=in_specs,
        out_specs=anywhere,
        scratch_shapes=[pltpu.VMEM((count, ROWS, COLS), jnp.float32), pltpu.SemaphoreType.DMA((count,))],
        input_output_aliases=aliases,
        compiler_params=pltpu.CompilerParams(vmem_limit_bytes=LIMIT),
        cost_estimate=pl.CostEstimate(flops=count * ROWS, bytes_accessed=count * ROWS, transcendentals=0),
    )(*args)


def pair_weights(occ_level, virt_level):
    energy_gap = 0.01 * (virt_level - occ_level).astype(jnp.float32)
    return -4.0 * energy_gap / (energy_gap * energy_gap + 1.0)


def per_device(mantissa, exponent, occ_level, virt_level):
    row, col = lax.axis_index("prow"), lax.axis_index("pcol")

    own = dequantize(mantissa, exponent)
    same_x = [[4 * x + i for i in range(4)] for x in range(NX)]
    group = lax.all_gather(own, "prow", axis=0, tiled=True, axis_index_groups=same_x)

    placed = send(group, spread())
    along_x = [[4 * x + i for x in range(NX)] for i in range(4)]
    groups = lax.all_to_all(
        jnp.broadcast_to(group, (NX, *group.shape)), "prow", 0, 0, axis_index_groups=along_x
    )
    down = send(placed, shift(dz=1))
    up = send(placed, shift(dz=-1))
    over = send(placed, shift(dy=2))
    weights = pair_weights(occ_level, virt_level)[None, :]
    columns = scale(weights, groups.reshape(COLS, DEPTH))
    steps = jnp.array([0, 1, 4, 7, 2, 5, 6, 3], jnp.int32)
    order = jnp.take(jnp.asarray(chunk_table()), row * CHUNKS + (color_of(row, col) + steps) % CHUNKS)
    over_up = send(up, shift(dy=2))
    over_down = send(down, shift(dy=2))
    up_two = send(up, shift(dz=-1))
    down_two = send(down, shift(dz=1))

    response = multiply(0, order, columns, [placed, up, over], None)
    response = multiply(3, order, columns, [down], response)
    response = multiply(4, order, columns, [up_two, over_up], response)
    response = multiply(6, order, columns, [down_two], response)
    response = multiply(7, order, columns, [over_down], response)
    return response.reshape(CHUNKS * ROWS, COLS)


def solution(mesh):
    return jax.shard_map(
        per_device,
        mesh=mesh,
        in_specs=(P(("pcol", "prow"), None), P(("pcol", "prow"), None), P(), P()),
        out_specs=P("prow", "pcol"),
        check_vma=False,
    )
```

```python
import jax
import jax.numpy as jnp
import numpy as np
from jax import lax
from jax.experimental import pallas as pl
from jax.experimental.pallas import tpu as pltpu
from jax.sharding import PartitionSpec as P

NX, NY, NZ = 4, 4, 16
ROWS = 160
CHUNKS = 8
DEPTH = 1024
COLS = 640
JOINT = ("prow", "pcol")
LIMIT = 32 * 1024 * 1024

PLACES = (
    (6, 14, 26, 18, 9, 1, 21, 29, 5, 13, 25, 17, 2, 10, 22, 30, 12, 4, 24, 16, 0, 8, 28, 20, 3, 11, 23, 31, 15, 7, 19, 27),
    (15, 7, 19, 27, 3, 11, 23, 31, 0, 8, 28, 20, 4, 12, 16, 24, 13, 5, 25, 17, 10, 2, 22, 30, 6, 14, 26, 18, 1, 9, 21, 29),
    (17, 25, 13, 5, 30, 22, 2, 10, 26, 18, 14, 6, 21, 29, 1, 9, 24, 16, 4, 12, 28, 20, 0, 8, 19, 27, 15, 7, 23, 31, 3, 11),
    (19, 27, 7, 15, 23, 31, 11, 3, 16, 24, 4, 12, 28, 20, 8, 0, 30, 22, 10, 2, 21, 29, 9, 1, 25, 17, 5, 13, 26, 18, 6, 14),
    (2, 10, 30, 22, 1, 9, 29, 21, 5, 13, 25, 17, 6, 14, 26, 18, 4, 12, 16, 24, 8, 0, 20, 28, 11, 3, 23, 31, 15, 7, 27, 19),
    (15, 7, 27, 19, 11, 3, 23, 31, 0, 8, 20, 28, 4, 12, 16, 24, 13, 5, 25, 17, 2, 10, 30, 22, 14, 6, 26, 18, 1, 9, 29, 21),
    (18, 26, 14, 6, 22, 30, 10, 2, 17, 25, 13, 5, 29, 21, 1, 9, 16, 24, 12, 4, 28, 20, 0, 8, 31, 23, 3, 11, 27, 19, 15, 7),
    (19, 27, 15, 7, 31, 23, 11, 3, 28, 20, 8, 0, 24, 16, 12, 4, 17, 25, 13, 5, 21, 29, 1, 9, 26, 18, 14, 6, 22, 30, 2, 10),
    (18, 26, 14, 6, 29, 21, 1, 9, 22, 30, 10, 2, 25, 17, 5, 13, 31, 23, 11, 3, 19, 27, 7, 15, 16, 24, 12, 4, 20, 28, 0, 8),
    (28, 20, 8, 0, 24, 16, 12, 4, 19, 27, 7, 15, 23, 31, 11, 3, 30, 22, 10, 2, 17, 25, 5, 13, 29, 21, 1, 9, 18, 26, 6, 14),
    (1, 9, 29, 21, 6, 14, 18, 26, 2, 10, 22, 30, 13, 5, 25, 17, 0, 8, 20, 28, 4, 12, 24, 16, 7, 15, 19, 27, 3, 11, 31, 23),
    (3, 11, 23, 31, 15, 7, 19, 27, 4, 12, 24, 16, 0, 8, 28, 20, 5, 13, 17, 25, 2, 10, 30, 22, 9, 1, 29, 21, 14, 6, 26, 18),
    (17, 25, 13, 5, 29, 21, 9, 1, 30, 22, 2, 10, 18, 26, 14, 6, 28, 20, 0, 8, 24, 16, 4, 12, 19, 27, 15, 7, 23, 31, 11, 3),
    (31, 23, 11, 3, 27, 19, 7, 15, 16, 24, 12, 4, 28, 20, 0, 8, 26, 18, 14, 6, 22, 30, 2, 10, 21, 29, 9, 1, 25, 17, 5, 13),
    (14, 6, 26, 18, 9, 1, 29, 21, 2, 10, 22, 30, 13, 5, 25, 17, 0, 8, 20, 28, 4, 12, 24, 16, 15, 7, 27, 19, 11, 3, 31, 23),
    (11, 3, 31, 23, 15, 7, 19, 27, 12, 4, 24, 16, 8, 0, 28, 20, 13, 5, 25, 17, 10, 2, 30, 22, 9, 1, 21, 29, 14, 6, 26, 18),
)


def color_of(row, col):
    return (col % NZ + 4 * (col // NZ) - 2 * row) % CHUNKS


def chunk_table():
    table = np.zeros((16, CHUNKS), np.int32)
    for row, places in enumerate(PLACES):
        for slot, col in enumerate(places):
            table[row, color_of(row, col)] = slot // 4
    return table


def split(index):
    row, col = divmod(index, 2 * NZ)
    return row >> 2, (col // NZ) * 2 + ((row >> 1) & 1), col % NZ, row & 1


def join(x, y, z, core):
    x, y, z = x % NX, y % NY, z % NZ
    return (x * 4 + (y & 1) * 2 + core) * 2 * NZ + (y >> 1) * NZ + z


def shift(dx=0, dy=0, dz=0):
    pairs = []
    for source in range(2 * NX * NY * NZ):
        x, y, z, core = split(source)
        pairs.append((source, join(x + dx, y + dy, z + dz, core)))
    return pairs


def spread():
    pairs = []
    for source in range(2 * NX * NY * NZ):
        x, y, z, core = split(source)
        col = (y >> 1) * NZ + z
        row, half = col // 2, col % 2
        place = PLACES[row][4 * (4 * half + x) + 2 * (y & 1) + core]
        pairs.append((source, row * 2 * NZ + place))
    return pairs


def send(block, pairs):
    return lax.ppermute(block, JOINT, pairs)


def dequantize_body(mantissa, exponent, out):
    scale = jnp.exp2(exponent[...].astype(jnp.float32)).T
    for k in range(DEPTH // 128):
        span = slice(128 * k, 128 * (k + 1))
        out[:, span] = (mantissa[:, span].astype(jnp.float32) * scale[:, k : k + 1]).astype(jnp.bfloat16)


def dequantize(mantissa, exponent):
    whole = pl.BlockSpec(memory_space=pltpu.VMEM)
    return pl.pallas_call(
        dequantize_body,
        out_shape=jax.ShapeDtypeStruct(mantissa.shape, jnp.bfloat16),
        in_specs=[whole, whole],
        out_specs=whole,
        compiler_params=pltpu.CompilerParams(vmem_limit_bytes=LIMIT),
    )(mantissa, exponent.T)


def scale_body(weights, rows, out):
    for k in range(DEPTH // 256):
        span = slice(256 * k, 256 * (k + 1))
        out[span, :] = (rows[:, span].astype(jnp.float32) * weights[:, span]).astype(jnp.bfloat16).T


def scale(weights, rows):
    whole = pl.BlockSpec(memory_space=pltpu.VMEM)
    return pl.pallas_call(
        scale_body,
        out_shape=jax.ShapeDtypeStruct((DEPTH, COLS), jnp.bfloat16),
        in_specs=[whole, whole],
        out_specs=whole,
        compiler_params=pltpu.CompilerParams(vmem_limit_bytes=LIMIT),
        cost_estimate=pl.CostEstimate(flops=COLS, bytes_accessed=COLS, transcendentals=0),
    )(weights, rows)


def multiply_body(first, order, columns, *rest):
    *blocks, response, held, sems = rest
    copies = []
    for block in blocks:
        for k in range(block.shape[0] // ROWS):
            slot = len(copies)
            held[slot] = jnp.dot(
                block[ROWS * k : ROWS * (k + 1), :], columns[...], preferred_element_type=jnp.float32
            )
            copies.append(pltpu.make_async_copy(held.at[slot], response.at[order[first + slot]], sems.at[slot]))
            copies[-1].start()
    for copy in copies:
        copy.wait()


def multiply(first, order, columns, blocks, response):
    count = sum(block.shape[0] for block in blocks) // ROWS
    whole = pl.BlockSpec(memory_space=pltpu.VMEM)
    anywhere = pl.BlockSpec(memory_space=pl.ANY)
    in_specs = [pl.BlockSpec(memory_space=pltpu.SMEM)] + [whole] * (1 + len(blocks))
    args = [order, columns, *blocks]
    aliases = {}

    def body(*refs):
        if response is not None:
            refs = refs[: len(args) - 1] + refs[len(args) :]
        multiply_body(first, *refs)

    if response is not None:
        in_specs.append(anywhere)
        args.append(response)
        aliases = {len(args) - 1: 0}
    return pl.pallas_call(
        body,
        out_shape=jax.ShapeDtypeStruct((CHUNKS, ROWS, COLS), jnp.float32),
        in_specs=in_specs,
        out_specs=anywhere,
        scratch_shapes=[pltpu.VMEM((count, ROWS, COLS), jnp.float32), pltpu.SemaphoreType.DMA((count,))],
        input_output_aliases=aliases,
        compiler_params=pltpu.CompilerParams(vmem_limit_bytes=LIMIT),
        cost_estimate=pl.CostEstimate(flops=count * ROWS, bytes_accessed=count * ROWS, transcendentals=0),
    )(*args)


def pair_weights(occ_level, virt_level):
    energy_gap = 0.01 * (virt_level - occ_level).astype(jnp.float32)
    return -4.0 * energy_gap / (energy_gap * energy_gap + 1.0)


def per_device(mantissa, exponent, occ_level, virt_level):
    row, col = lax.axis_index("prow"), lax.axis_index("pcol")

    own = dequantize(mantissa, exponent)
    same_x = [[4 * x + i for i in range(4)] for x in range(NX)]
    group = lax.all_gather(own, "prow", axis=0, tiled=True, axis_index_groups=same_x)

    placed = send(group, spread())
    along_x = [[4 * x + i for x in range(NX)] for i in range(4)]
    groups = lax.all_to_all(
        jnp.broadcast_to(group, (NX, *group.shape)), "prow", 0, 0, axis_index_groups=along_x
    )
    down = send(placed, shift(dz=1))
    up = send(placed, shift(dz=-1))
    over = send(placed, shift(dy=2))
    weights = pair_weights(occ_level, virt_level)[None, :]
    columns = scale(weights, groups.reshape(COLS, DEPTH))
    steps = jnp.array([0, 1, 4, 7, 2, 5, 6, 3], jnp.int32)
    order = jnp.take(jnp.asarray(chunk_table()), row * CHUNKS + (color_of(row, col) + steps) % CHUNKS)
    over_up = send(up, shift(dy=2))
    over_down = send(down, shift(dy=2))
    up_two = send(up, shift(dz=-1))
    down_two = send(down, shift(dz=1))

    response = multiply(0, order, columns, [placed, up, over], None)
    response = multiply(3, order, columns, [down], response)
    response = multiply(4, order, columns, [up_two, over_up], response)
    response = multiply(6, order, columns, [down_two], response)
    response = multiply(7, order, columns, [over_down], response)
    return response.reshape(CHUNKS * ROWS, COLS)


def solution(mesh):
    return jax.shard_map(
        per_device,
        mesh=mesh,
        in_specs=(P(("pcol", "prow"), None), P(("pcol", "prow"), None), P(), P()),
        out_specs=P("prow", "pcol"),
        check_vma=False,
    )
```
